32 devices in a mesh: dp: 8 (over z, core), help: 4 (over y, x).
Axes of the slice: x: 2, y: 2, z: 4, core: 2. Of those that a mesh axis runs over, the one named last changes fastest.
Arguments:
- queries: bfloat16 [8192, 16, 128], P(('dp', 'help')), may hold values from -48 to 48
- keys_values: bfloat16 [8192, 4, 256], P(('dp', 'help')), may hold values from -4 to 4
- segment_ids: int32 [8, 1024], P('dp', 'help'), may hold values from 0 to 3, never falling along the last dimension, each value on 1 to 512 neighbouring positions
- residual: bfloat16 [8192, 4096], P(('dp', 'help')), may hold values from -3 to 3
- out_weight: bfloat16 [2048, 4096], P(None, 'dp'), may hold values from -1 to 1
Outputs:
- layer_out: bfloat16 [8192, 4096], P(('dp', 'help'))
The draws below stay inside these ranges and needn't reach their ends.
All inputs are finite; a program needn't handle non-finite values.
Results may differ from the reference program's by a relative error of at most 0.0085.
Values may be sent and summed in bfloat16 or wider, within the bound.
A program may use at most 128 MiB of HBM per device.

```python
import math
import jax
import jax.numpy as jnp
import numpy as np
from jax import lax

D = 4096
HEAD_DIM = 128
HEADS = 16
KV_HEADS = 4
COUNT = 4
ROW = 1024
MOST = 512
ROWS = 8
TOKENS = 8192


def paired_draw(key):
    base = jax.random.fold_in(key, 911)
    key_query, key_pairs = jax.random.split(base, 2)
    queries = jnp.clip(jax.random.normal(key_query, (TOKENS, HEADS, HEAD_DIM), jnp.float32), -4.0, 4.0)
    pairs = jnp.clip(jax.random.normal(key_pairs, (TOKENS, KV_HEADS, 2 * HEAD_DIM), jnp.float32), -4.0, 4.0)
    return (queries, pairs)


def draw_queries(key, part):
    return paired_draw(key)[0].astype(jnp.bfloat16)


def draw_keys_values(key, part):
    return paired_draw(key)[1].astype(jnp.bfloat16)


def block_levels(rng, extent, pieces, smallest, high):
    loudness = 1.0
    for position, parts in pieces:
        steps = jax.random.uniform(jax.random.fold_in(jax.random.fold_in(rng, 6), position), (parts,), jnp.float32, smallest / len(pieces), high / len(pieces))
        loudness = loudness * jnp.repeat(jnp.exp(steps), extent[position] // parts).reshape((-1,) + (1,) * (len(extent) - 1 - position))
    return loudness


def profile(amount, total, most, slope):
    loads = [(1 << 20) // math.isqrt(rank ** slope) + 1 for rank in range(2, amount + 1)]
    surplus, counts = total - most - (amount - 1), [1] * (amount - 1)
    while surplus > 0:
        candidates = [i for i in range(amount - 1) if counts[i] < most]
        mass, remaining = sum([loads[i] for i in candidates]), surplus
        for i in candidates:
            addition = min(most - counts[i], max(1, remaining * loads[i] // mass), surplus)
            counts[i] = counts[i] + addition
            surplus = surplus - addition
    return np.array([most] + counts)


def uneven(own_key, number_of, total, reach, lean):
    if number_of == 2:
        one = jax.random.randint(own_key, (), max(1, total - reach), min(reach, total - 1) + 1)
        return jnp.stack([one, total - one])
    tallies = jnp.asarray(profile(number_of, total, reach, lean), jnp.int32)
    twos = (number_of - 1) // 2
    giver, receiver = tallies[1:1 + 2 * twos:2], tallies[2:2 + 2 * twos:2]
    room = jnp.minimum(giver - 1, reach - receiver)
    passed = jax.random.randint(jax.random.fold_in(own_key, 1), (twos,), 0, 1 << 20) % (room + 1)
    tallies = tallies.at[1:1 + 2 * twos:2].set(giver - passed).at[2:2 + 2 * twos:2].set(receiver + passed)
    return tallies[jax.random.permutation(jax.random.fold_in(own_key, 2), number_of)]


def gaussian(rng, shape, spread, most, cuts=(), kind=jnp.bfloat16):
    values = spread * jax.random.normal(rng, shape, jnp.float32)
    if cuts:
        values = values * block_levels(rng, shape, cuts, -0.22, 0.18)
    return jnp.clip(values, -most, most).astype(kind)


def setup_inputs(seed: int = 0) -> dict:
    arg_keys = jax.random.split(jax.random.key(seed), 6)
    return {
        "queries": draw_queries(jax.random.fold_in(arg_keys[5], 71), 0),
        "keys_values": draw_keys_values(jax.random.fold_in(arg_keys[5], 71), 0),
        "segment_ids": jax.vmap(lambda own: jnp.searchsorted(jnp.cumsum(uneven(own, COUNT, ROW, MOST, 2)), jnp.arange(ROW), side="right"))(jax.random.split(arg_keys[2], ROWS)).reshape((ROWS, ROW)).astype(jnp.int32),
        "residual": gaussian(arg_keys[3], (TOKENS, D), 0.5, 3.0, ((0, 32),)),
        "out_weight": gaussian(arg_keys[4], (HEADS * HEAD_DIM, D), (HEADS * HEAD_DIM // 64) ** -0.5, 1.0, ((1, 8),)),
    }


masked_score = -1e+30

def reference(queries, keys_values, segment_ids, residual, out_weight):
    group_size = HEADS // KV_HEADS
    score_scale = 1.0 / math.sqrt(HEAD_DIM)
    block_rows = min(512, ROW)
    window = min(MOST + block_rows, ROW)
    query_blocks = ROW // block_rows
    row_queries = queries.reshape(ROWS, ROW, HEADS, HEAD_DIM)
    row_keys = keys_values.reshape(ROWS, ROW, KV_HEADS, 2 * HEAD_DIM)
    row_stream = residual.reshape(ROWS, ROW, D)

    def one_row(row_inputs):
        row_q, row_kv, row_seg, row_res = row_inputs

        def one_block(block_index):
            query_start = (block_index * block_rows).astype(jnp.int32)
            key_start = jnp.clip(query_start + block_rows - window, 0, ROW - window).astype(jnp.int32)
            block_q = lax.dynamic_slice_in_dim(row_q, query_start, block_rows, 0)
            block_q = block_q.reshape(block_rows, KV_HEADS, group_size, HEAD_DIM).astype(jnp.float32)
            block_kv = lax.dynamic_slice_in_dim(row_kv, key_start, window, 0).astype(jnp.float32)
            keys = block_kv[..., :HEAD_DIM]
            values = block_kv[..., HEAD_DIM:]
            query_pos = query_start + jnp.arange(block_rows, dtype=jnp.int32)
            key_pos = key_start + jnp.arange(window, dtype=jnp.int32)
            query_seg = lax.dynamic_slice_in_dim(row_seg, query_start, block_rows, 0)
            key_seg = lax.dynamic_slice_in_dim(row_seg, key_start, window, 0)
            allowed = (key_pos[None, :] <= query_pos[:, None]) & (key_seg[None, :] == query_seg[:, None])
            scores = jnp.einsum('qhgd,thd->hgqt', block_q, keys) * score_scale
            scores = jnp.where(allowed, scores, masked_score)
            maxima = lax.optimization_barrier(jnp.max(scores, axis=-1, keepdims=True))
            weights = jnp.where(allowed, jnp.exp(scores - maxima), 0.0)
            totals = lax.optimization_barrier(jnp.sum(weights, axis=-1))
            rounded = lax.optimization_barrier(weights.astype(jnp.bfloat16)).astype(jnp.float32)
            mixed = jnp.einsum('hgqt,thd->qhgd', rounded, values)
            result = mixed / jnp.transpose(totals, (2, 0, 1))[..., None]
            return result.astype(jnp.bfloat16).reshape(block_rows, HEADS * HEAD_DIM)
        attended = lax.map(one_block, jnp.arange(query_blocks, dtype=jnp.int32)).reshape(ROW, HEADS * HEAD_DIM)
        projected = jnp.dot(attended, out_weight, preferred_element_type=jnp.float32)
        return (row_res.astype(jnp.float32) + projected).astype(jnp.bfloat16)
    layer_out = lax.map(one_row, (row_queries, row_keys, segment_ids, row_stream))
    return layer_out.reshape(TOKENS, D)
```

```python
import functools
import math

import jax
import jax.numpy as jnp
from jax import lax
from jax.experimental import pallas as pl
from jax.experimental.pallas import tpu as pltpu
from jax.sharding import PartitionSpec as P

MESH = pl.DeviceIdType.MESH
masked_score = -1e30


def kernel(
    dims,
    q_ref,
    kv_ref,
    segr_ref,
    segc_ref,
    res_ref,
    w_ref,
    out_ref,
    wbuf,
    kvbuf,
    segbuf,
    qbuf,
    att,
    resbuf,
    ost,
    w_recv,
    z_send,
    p_send,
    kv_recv,
    kv_send,
    seg_recv,
    seg_send,
    res_recv,
    res_send,
    att_recv,
    att_send,
    out_recv,
    out_send,
    loc,
    loc_out,
):
    nz, ny, nx, back, heads, heads_kv, hd, rows, cols, width = dims
    nh = ny * nx
    quarter = width // nh
    piece_rows = quarter // 2
    dp = lax.axis_index("dp")
    h = lax.axis_index("help")
    z, c = dp // 2, lax.rem(dp, 2)
    y, x = h // nx, lax.rem(h, nx)
    sib = (z * 2 + (1 - c), h)
    x_mates = [lax.rem(x + i, nx) for i in range(1, nx)]
    y_mates = [lax.rem(y + i, ny) for i in range(1, ny)]

    def column(zp, core):
        return pl.ds(pl.multiple_of((zp * 2 + core) * cols, cols), cols)

    def own_rows(core):
        return pl.ds(pl.multiple_of(core * rows, rows), rows)

    def piece(zp, hp, half):
        start = pl.multiple_of(hp * quarter + half * piece_rows, piece_rows)
        return wbuf.at[zp, pl.ds(start, piece_rows)]

    def remote(src, dst, ssem, rsem, dev):
        return pltpu.make_async_remote_copy(
            src_ref=src, dst_ref=dst, send_sem=ssem, recv_sem=rsem, device_id=dev, device_id_type=MESH
        )

    barrier = pltpu.get_barrier_semaphore()
    greet = functools.partial(pl.semaphore_signal, barrier, inc=1, device_id_type=MESH)
    greet(device_id=sib)
    for i in range(1, nh):
        greet(device_id=(dp, lax.rem(h + i, nh)))

    @pl.when(z > 0)
    def _():
        greet(device_id=(dp - 2, h))

    @pl.when(z < nz - 1)
    def _():
        greet(device_id=(dp + 2, h))

    pl.semaphore_wait(
        barrier, nh + jnp.where(z > 0, 1, 0) + jnp.where(z < nz - 1, 1, 0)
    )

    def z_copy(src, zp, half, way, step):
        dev = (dp + 2, h) if way == 0 else (dp - 2, h)
        return remote(src, piece(zp, h, half), z_send.at[way, step, half], w_recv.at[zp, h, half], dev)

    def own_piece(half):
        start = pl.multiple_of(h * quarter + half * piece_rows, piece_rows)
        return w_ref.at[pl.ds(start, piece_rows)]

    for half in range(2):

        @pl.when(z < nz - 1)
        def _(half=half):
            z_copy(own_piece(half), z, half, 0, 0).start()

        @pl.when(z > 0)
        def _(half=half):
            z_copy(own_piece(half), z, half, 1, 0).start()

    def seg_copy(j):
        return remote(segr_ref, segbuf.at[j], seg_send.at[j], seg_recv.at[j], (dp, lax.rem(h + j, nh)))

    def kv_copy(j, g):
        return remote(
            kv_ref.at[g], kvbuf.at[j, g], kv_send.at[j, g], kv_recv.at[j, g], (dp, lax.rem(h + j, nh))
        )

    for j in range(1, back + 1):

        @pl.when(h + j < nh)
        def _(j=j):
            seg_copy(j).start()

    for g in range(heads_kv):
        for j in range(1, back + 1):

            @pl.when(h + j < nh)
            def _(j=j, g=g):
                kv_copy(j, g).start()

    local = [
        pltpu.make_async_copy(q_ref, qbuf, loc.at[0]),
        pltpu.make_async_copy(kv_ref, kvbuf.at[0], loc.at[1]),
        pltpu.make_async_copy(segr_ref, segbuf.at[0], loc.at[2]),
        pltpu.make_async_copy(w_ref, wbuf.at[z], loc.at[3]),
    ]
    for copy in local:
        copy.start()

    def res_copy(zp):
        return remote(
            res_ref.at[:, column(zp, 1 - c)],
            resbuf.at[zp, own_rows(c)],
            res_send.at[zp],
            res_recv.at[zp],
            sib,
        )

    def res_local(zp):
        return pltpu.make_async_copy(
            res_ref.at[:, column(zp, c)], resbuf.at[zp, own_rows(c)], loc.at[4 + zp]
        )

    for zp in range(nz):
        res_copy(zp).start()
        res_local(zp).start()

    def both_ways(step, run):
        @pl.when(z >= step)
        def _():
            run(z - step, 0)

        @pl.when(z + step < nz)
        def _():
            run(z + step, 1)

    def to_x(zp, hp, half):
        for xm in x_mates:
            remote(
                piece(zp, hp, half), piece(zp, hp, half), p_send.at[zp], w_recv.at[zp, hp, half], (dp, y * nx + xm)
            ).start()

    def to_y(zp, hp, half):
        for ym in y_mates:
            remote(
                piece(zp, hp, half), piece(zp, hp, half), p_send.at[zp], w_recv.at[zp, hp, half], (dp, ym * nx + x)
            ).start()

    def arrived(zp, hp, half):
        remote(
            piece(zp, hp, half), piece(zp, hp, half), p_send.at[zp], w_recv.at[zp, hp, half], sib
        ).wait_recv()

    def from_z(step, half):
        def run(zp, way):
            arrived(zp, h, half)

            @pl.when((z < nz - 1) if way == 0 else (z > 0))
            def _():
                z_copy(piece(zp, h, half), zp, half, way, step).start()

            to_x(zp, h, half)
            to_y(zp, h, half)

        both_ways(step, run)

    def relay(step):
        def run(zp, way):
            for xm in x_mates:
                arrived(zp, y * nx + xm, 0)
                to_y(zp, y * nx + xm, 0)
            for ym in y_mates:
                arrived(zp, ym * nx + x, 1)
                to_x(zp, ym * nx + x, 1)

        both_ways(step, run)

    scale = 1.0 / math.sqrt(hd)
    group = heads // heads_kv
    per_chunk = 2

    def attend(g, first):
        if first == 0:
            for j in range(1, back + 1):

                @pl.when(h >= j)
                def _(j=j):
                    if g == 0:
                        seg_copy(j).wait_recv()
                    kv_copy(j, g).wait_recv()

        q_seg = segc_ref[...]
        here = [g * group + first + i for i in range(per_chunk)]

        def scores(head, j, allowed):
            s = lax.dot_general(
                qbuf[head], kvbuf[j, g, :, 0:hd], (((1,), (1,)), ((), ())), preferred_element_type=jnp.float32
            )
            return jnp.where(allowed, s * scale, masked_score)

        def mix(weights, j):
            return jnp.dot(
                weights.astype(jnp.bfloat16), kvbuf[j, g, :, hd:], preferred_element_type=jnp.float32
            )

        same = q_seg == segbuf[0, 0:1, :]
        causal = lax.broadcasted_iota(jnp.int32, (rows, rows), 1) <= lax.broadcasted_iota(
            jnp.int32, (rows, rows), 0
        )
        states = []
        for head in here:
            s = scores(head, 0, same & causal)
            top = jnp.max(s, axis=-1, keepdims=True)
            weights = jnp.exp(s - top)
            states.append((top, jnp.sum(weights, axis=-1, keepdims=True), mix(weights, 0)))

        def earlier(j, states):
            allowed = q_seg == segbuf[j, 0:1, :]
            after = []
            for head, (top, total, running) in zip(here, states):
                s = scores(head, j, allowed)
                new_top = jnp.maximum(top, jnp.max(s, axis=-1, keepdims=True))
                weights = jnp.exp(s - new_top)
                factor = jnp.exp(top - new_top)
                total = total * factor + jnp.sum(weights, axis=-1, keepdims=True)
                after.append((new_top, total, running * factor + mix(weights, j)))
            return tuple(after)

        states = lax.fori_loop(1, jnp.minimum(h, back) + 1, earlier, tuple(states))
        for head, (top, total, running) in zip(here, states):
            att[own_rows(c), head * hd : (head + 1) * hd] = (running / total).astype(jnp.bfloat16)

    def att_copy(core):
        return remote(att.at[own_rows(core)], att.at[own_rows(core)], att_send, att_recv, sib)

    tile = min(256, cols)

    def out_local(zp):
        return pltpu.make_async_copy(
            ost.at[zp, own_rows(c)], out_ref.at[:, column(zp, c)], loc_out.at[zp]
        )

    def out_copy(zp, core):
        return remote(
            ost.at[zp, own_rows(1 - c)], out_ref.at[:, column(zp, core)], out_send.at[zp], out_recv.at[zp], sib
        )

    def project(zp, way):
        @pl.loop(0, cols // tile)
        def _(n):
            part = pl.ds(pl.multiple_of(n * tile, tile), tile)
            summed = jnp.dot(att[...], wbuf[zp, :, part], preferred_element_type=jnp.float32)
            ost[zp, :, part] = (resbuf[zp, :, part].astype(jnp.float32) + summed).astype(jnp.bfloat16)

        out_copy(zp, c).start()
        out_local(zp).start()

    def complete(zp):
        for xm in x_mates:
            arrived(zp, y * nx + xm, 1)
        for ym in y_mates:
            arrived(zp, ym * nx + x, 0)
        for ym in y_mates:
            for xm in x_mates:
                arrived(zp, ym * nx + xm, 0)
                arrived(zp, ym * nx + xm, 1)

    for copy in local[:3]:
        copy.wait()
    work = [
        functools.partial(attend, g, first)
        for g in range(heads_kv)
        for first in range(0, group, per_chunk)
    ]

    def compute(count):
        for _ in range(count):
            if work:
                work.pop(0)()

    compute(1)
    for step in range(1, nz):
        from_z(step, 0)
        compute(1)
        from_z(step, 1)
        compute(1)
        relay(step)
        compute(2)
        if step == 2 or nz <= 2:
            compute(len(work))
            att_copy(c).start()
            local[3].wait()
            for zp in range(nz):
                res_local(zp).wait()
                res_copy(zp).wait_recv()
            att_copy(1 - c).wait_recv()
            project(z, 0)

    for step in range(1, nz):

        def run(zp, way):
            complete(zp)
            project(zp, way)

        both_ways(step, run)

    for zp in range(nz):
        out_local(zp).wait()
        out_copy(zp, c).wait_send()
        out_copy(zp, 1 - c).wait_recv()
        res_copy(zp).wait_send()
    att_copy(c).wait_send()
    for j in range(1, back + 1):

        @pl.when(h + j < nh)
        def _(j=j):
            seg_copy(j).wait_send()
            for g in range(heads_kv):
                kv_copy(j, g).wait_send()

    for half in range(2):

        @pl.when(z < nz - 1)
        def _(half=half):
            z_copy(own_piece(half), z, half, 0, 0).wait_send()

        @pl.when(z > 0)
        def _(half=half):
            z_copy(own_piece(half), z, half, 1, 0).wait_send()

    for step in range(1, nz):

        def drain(zp, way):
            for half in range(2):

                @pl.when((z < nz - 1) if way == 0 else (z > 0))
                def _(half=half):
                    z_copy(piece(zp, h, half), zp, half, way, step).wait_send()

            if nh > 1:
                sent = wbuf.at[zp, 0 : quarter * (nh - 1)]
                pltpu.make_async_copy(sent, sent, p_send.at[zp]).wait()

        both_ways(step, drain)


def on_device(ndp, nh, queries, keys_values, segment_ids, residual, out_weight):
    rows, heads, hd = queries.shape
    heads_kv = keys_values.shape[1]
    width, cols = out_weight.shape
    nz = ndp // 2
    nx = math.isqrt(nh)
    while nh % nx:
        nx -= 1
    ny = nh // nx
    back = nh // 2
    dims = (nz, ny, nx, back, heads, heads_kv, hd, rows, cols, width)
    seg = segment_ids.reshape(rows)
    any_spec = pl.BlockSpec(memory_space=pl.ANY)
    dma = pltpu.SemaphoreType.DMA
    bf16 = jnp.bfloat16
    return pl.pallas_call(
        functools.partial(kernel, dims),
        out_shape=jax.ShapeDtypeStruct(residual.shape, bf16),
        in_specs=[any_spec, any_spec, any_spec, pl.BlockSpec(memory_space=pltpu.VMEM), any_spec, any_spec],
        out_specs=any_spec,
        scratch_shapes=[
            pltpu.VMEM((nz, width, cols), bf16),
            pltpu.VMEM((back + 1, heads_kv, rows, 2 * hd), bf16),
            pltpu.VMEM((back + 1, 8, rows), jnp.int32),
            pltpu.VMEM((heads, rows, hd), bf16),
            pltpu.VMEM((2 * rows, width), bf16),
            pltpu.VMEM((nz, 2 * rows, cols), bf16),
            pltpu.VMEM((nz, 2 * rows, cols), bf16),
            dma((nz, nh, 2)),
            dma((2, nz, 2)),
            dma((nz,)),
            dma((back + 1, heads_kv)),
            dma((back + 1, heads_kv)),
            dma((back + 1,)),
            dma((back + 1,)),
            dma((nz,)),
            dma((nz,)),
            dma,
            dma,
            dma((nz,)),
            dma((nz,)),
            dma((4 + nz,)),
            dma((nz,)),
        ],
        compiler_params=pltpu.CompilerParams(
            collective_id=0, has_side_effects=True, vmem_limit_bytes=56 * 1024 * 1024
        ),
        cost_estimate=pl.CostEstimate(flops=6 * 10**9, bytes_accessed=2 * 10**7, transcendentals=3 * 10**6),
    )(
        jnp.transpose(queries, (1, 0, 2)),
        jnp.transpose(keys_values, (1, 0, 2)),
        jnp.broadcast_to(seg[None, :], (8, rows)),
        seg[:, None],
        residual,
        out_weight,
    )


def solution(mesh):
    return jax.shard_map(
        functools.partial(on_device, mesh.shape["dp"], mesh.shape["help"]),
        mesh=mesh,
        in_specs=(
            P(("dp", "help"), None, None),
            P(("dp", "help"), None, None),
            P("dp", "help"),
            P(("dp", "help"), None),
            P(None, "dp"),
        ),
        out_specs=P(("dp", "help"), None),
        check_vma=False,
    )
```

```python
import functools
import math

import jax
import jax.numpy as jnp
from jax import lax
from jax.experimental import pallas as pl
from jax.experimental.pallas import tpu as pltpu
from jax.sharding import PartitionSpec as P

MESH = pl.DeviceIdType.MESH
masked_score = -1e30


def kernel(
    dims,
    q_ref,
    kv_ref,
    seg_ref,
    res_ref,
    w_ref,
    out_ref,
    wbuf,
    kvbuf,
    segbuf,
    segcol,
    qraw,
    qbuf,
    att,
    resbuf,
    ost,
    w_recv,
    z_send,
    p_send,
    kv_recv,
    kv_send,
    relay_send,
    seg_recv,
    seg_send,
    res_recv,
    res_send,
    att_recv,
    att_send,
    out_recv,
    out_send,
    loc,
    loc_out,
):
    nz, ny, nx, back, heads, heads_kv, hd, rows, cols, width, direct, relays = dims
    nh = ny * nx
    quarter = (width - direct) // nh
    split = quarter // 32 * 16
    sizes = (split, quarter - split, direct)
    dp = lax.axis_index("dp")
    h = lax.axis_index("help")
    z, c = dp // 2, lax.rem(dp, 2)
    y, x = h // nx, lax.rem(h, nx)
    sib = (z * 2 + (1 - c), h)
    x_mates = [lax.rem(x + i, nx) for i in range(1, nx)]
    y_mates = [lax.rem(y + i, ny) for i in range(1, ny)]

    def column(zp, core):
        return pl.ds(pl.multiple_of((zp * 2 + core) * cols, cols), cols)

    def own_rows(core):
        return pl.ds(pl.multiple_of(core * rows, rows), rows)

    def piece(zp, hp, half):
        if half == 2:
            return wbuf.at[zp, 0:direct]
        start = pl.multiple_of(direct + hp * quarter + half * split, 16)
        return wbuf.at[zp, pl.ds(start, sizes[half])]

    def w_sem(zp, hp, half):
        return w_recv.at[zp, nh, 0] if half == 2 else w_recv.at[zp, hp, half]

    def remote(src, dst, ssem, rsem, dev):
        return pltpu.make_async_remote_copy(
            src_ref=src, dst_ref=dst, send_sem=ssem, recv_sem=rsem, device_id=dev, device_id_type=MESH
        )

    barrier = pltpu.get_barrier_semaphore()
    greet = functools.partial(pl.semaphore_signal, barrier, inc=1, device_id_type=MESH)
    greet(device_id=sib)
    for i in range(1, nh):
        greet(device_id=(dp, lax.rem(h + i, nh)))

    @pl.when(z > 0)
    def _():
        greet(device_id=(dp - 2, h))

    @pl.when(z < nz - 1)
    def _():
        greet(device_id=(dp + 2, h))

    pl.semaphore_wait(
        barrier, nh + jnp.where(z > 0, 1, 0) + jnp.where(z < nz - 1, 1, 0)
    )

    def z_copy(src, zp, half, way, step):
        dev = (dp + 2, h) if way == 0 else (dp - 2, h)
        return remote(src, piece(zp, h, half), z_send.at[way, step, half], w_sem(zp, h, half), dev)

    def own_piece(half):
        if half == 2:
            return w_ref.at[0:direct]
        start = pl.multiple_of(direct + h * quarter + half * split, 16)
        return w_ref.at[pl.ds(start, sizes[half])]

    def own_out(half):
        @pl.when(z < nz - 1)
        def _():
            z_copy(own_piece(half), z, half, 0, 0).start()

        @pl.when(z > 0)
        def _():
            z_copy(own_piece(half), z, half, 1, 0).start()

    own_out(0)
    own_out(1)

    def seg_copy(j):
        return remote(segbuf.at[0], segbuf.at[j], seg_send.at[j], seg_recv.at[j], (dp, lax.rem(h + j, nh)))

    def kv_copy(j, g):
        return remote(
            kv_ref.at[g], kvbuf.at[j, g], kv_send.at[j, g], kv_recv.at[j, g], (dp, lax.rem(h + j, nh))
        )

    def beside(j):
        if j % nx == 0:
            return h + j < nh
        return x + j < nx

    def relay_copy(i, g):
        j, t = relays[i]
        return remote(
            kvbuf.at[j, g], kvbuf.at[j + t, g], relay_send.at[i, g], kv_recv.at[j + t, g], (dp, lax.rem(h + t + nh, nh))
        )

    def relaying(i):
        j, t = relays[i]
        return (h >= j) & (x + t >= 0) & (x + t < nx)

    for g in range(heads_kv):
        for j in range(1, back + 1):

            @pl.when(beside(j))
            def _(j=j, g=g):
                kv_copy(j, g).start()

    segbuf[0] = jnp.broadcast_to(seg_ref[...], (8, rows))
    for j in range(1, back + 1):

        @pl.when(h + j < nh)
        def _(j=j):
            seg_copy(j).start()

    segcol[...] = jnp.transpose(jnp.broadcast_to(seg_ref[...], (128, rows)))

    local = [
        pltpu.make_async_copy(q_ref, qraw, loc.at[0]),
        pltpu.make_async_copy(kv_ref, kvbuf.at[0], loc.at[1]),
        pltpu.make_async_copy(w_ref, wbuf.at[z], loc.at[3]),
    ]
    for copy in local:
        copy.start()

    def res_copy(zp):
        return remote(
            res_ref.at[:, column(zp, 1 - c)],
            resbuf.at[zp, own_rows(c)],
            res_send.at[zp],
            res_recv.at[zp],
            sib,
        )

    def res_local(zp):
        return pltpu.make_async_copy(
            res_ref.at[:, column(zp, c)], resbuf.at[zp, own_rows(c)], loc.at[4 + zp]
        )

    for zp in range(nz):
        res_copy(zp).start()
        res_local(zp).start()

    def both_ways(step, run):
        @pl.when(z >= step)
        def _():
            run(z - step, 0)

        @pl.when(z + step < nz)
        def _():
            run(z + step, 1)

    def to_x(zp, hp, half):
        for xm in x_mates:
            remote(
                piece(zp, hp, half), piece(zp, hp, half), p_send.at[zp], w_sem(zp, hp, half), (dp, y * nx + xm)
            ).start()

    def to_y(zp, hp, half):
        for ym in y_mates:
            remote(
                piece(zp, hp, half), piece(zp, hp, half), p_send.at[zp], w_sem(zp, hp, half), (dp, ym * nx + x)
            ).start()

    def arrived(zp, hp, half):
        remote(
            piece(zp, hp, half), piece(zp, hp, half), p_send.at[zp], w_sem(zp, hp, half), sib
        ).wait_recv()

    def from_z(step, half):
        def run(zp, way):
            arrived(zp, h, half)

            @pl.when((z < nz - 1) if way == 0 else (z > 0))
            def _():
                z_copy(piece(zp, h, half), zp, half, way, step).start()

            if half < 2:
                to_x(zp, h, half)
                to_y(zp, h, half)

        both_ways(step, run)

    def relay(step):
        def run(zp, way):
            for xm in x_mates:
                arrived(zp, y * nx + xm, 0)
                to_y(zp, y * nx + xm, 0)
            for ym in y_mates:
                arrived(zp, ym * nx + x, 1)
                to_x(zp, ym * nx + x, 1)

        both_ways(step, run)

    scale = 1.0 / math.sqrt(hd)
    group = heads // heads_kv
    per_chunk = 2

    def fetch(g):
        for j in range(back, 0, -1):

            @pl.when(h >= j)
            def _(j=j):
                if g == 0:
                    seg_copy(j).wait_recv()
                kv_copy(j, g).wait_recv()

            for i, (held, _) in enumerate(relays):
                if held == j:

                    @pl.when(relaying(i))
                    def _(i=i):
                        relay_copy(i, g).start()

    def attend(g, first):
        if first + per_chunk >= group and g + 1 < heads_kv:
            fetch(g + 1)
        q_seg = segcol[:, 0:1]
        here = [g * group + first + i for i in range(per_chunk)]

        def scores(head, j, allowed):
            s = lax.dot_general(
                qbuf[head], kvbuf[j, g, :, 0:hd], (((1,), (1,)), ((), ())), preferred_element_type=jnp.float32
            )
            return jnp.where(allowed, s * scale, masked_score)

        def mix(weights, j):
            return jnp.dot(
                weights.astype(jnp.bfloat16), kvbuf[j, g, :, hd:], preferred_element_type=jnp.float32
            )

        same = q_seg == segbuf[0, 0:1, :]
        causal = lax.broadcasted_iota(jnp.int32, (rows, rows), 1) <= lax.broadcasted_iota(
            jnp.int32, (rows, rows), 0
        )
        states = []
        for head in here:
            s = scores(head, 0, same & causal)
            top = jnp.max(s, axis=-1, keepdims=True)
            weights = jnp.exp(s - top)
            states.append((top, jnp.sum(weights, axis=-1, keepdims=True), mix(weights, 0)))

        def earlier(j, states):
            allowed = q_seg == segbuf[j, 0:1, :]
            after = []
            for head, (top, total, running) in zip(here, states):
                s = scores(head, j, allowed)
                new_top = jnp.maximum(top, jnp.max(s, axis=-1, keepdims=True))
                weights = jnp.exp(s - new_top)
                factor = jnp.exp(top - new_top)
                total = total * factor + jnp.sum(weights, axis=-1, keepdims=True)
                after.append((new_top, total, running * factor + mix(weights, j)))
            return tuple(after)

        states = lax.fori_loop(1, jnp.minimum(h, back) + 1, earlier, tuple(states))
        for head, (top, total, running) in zip(here, states):
            att[own_rows(c), head * hd : (head + 1) * hd] = (running / total).astype(jnp.bfloat16)

    def att_copy(core):
        return remote(att.at[own_rows(core)], att.at[own_rows(core)], att_send, att_recv, sib)

    tile = min(256, cols)

    def out_local(zp):
        return pltpu.make_async_copy(
            ost.at[zp, own_rows(c)], out_ref.at[:, column(zp, c)], loc_out.at[zp]
        )

    def out_copy(zp, core):
        return remote(
            ost.at[zp, own_rows(1 - c)], out_ref.at[:, column(zp, core)], out_send.at[zp], out_recv.at[zp], sib
        )

    def project(zp, way):
        @pl.loop(0, cols // tile)
        def _(n):
            part = pl.ds(pl.multiple_of(n * tile, tile), tile)
            summed = jnp.dot(att[...], wbuf[zp, :, part], preferred_element_type=jnp.float32)
            ost[zp, :, part] = (resbuf[zp, :, part].astype(jnp.float32) + summed).astype(jnp.bfloat16)

        out_copy(zp, c).start()
        out_local(zp).start()

    def complete(zp):
        for xm in x_mates:
            arrived(zp, y * nx + xm, 1)
        for ym in y_mates:
            arrived(zp, ym * nx + x, 0)
        for ym in y_mates:
            for xm in x_mates:
                arrived(zp, ym * nx + xm, 0)
                arrived(zp, ym * nx + xm, 1)

    for copy in local[:2]:
        copy.wait()
    qbuf[...] = jnp.transpose(qraw[...], (1, 0, 2))
    fetch(0)
    work = [
        functools.partial(attend, g, first)
        for g in range(heads_kv)
        for first in range(0, group, per_chunk)
    ]

    def compute(count):
        for _ in range(count):
            if work:
                work.pop(0)()

    compute(1)
    for step in range(1, nz):
        from_z(step, 0)
        compute(1)
        from_z(step, 1)
        if step == 1:
            own_out(2)
        else:
            from_z(step - 1, 2)
        compute(1)
        relay(step)
        compute(2)
        if step == 2 or nz <= 2:
            compute(len(work))
            att_copy(c).start()
            local[2].wait()
            for zp in range(nz):
                res_local(zp).wait()
                res_copy(zp).wait_recv()
            att_copy(1 - c).wait_recv()
            project(z, 0)

    for step in range(1, nz):
        if step == nz - 1:
            from_z(step, 2)

        def run(zp, way):
            complete(zp)
            project(zp, way)

        both_ways(step, run)

    for zp in range(nz):
        out_local(zp).wait()
        out_copy(zp, c).wait_send()
        out_copy(zp, 1 - c).wait_recv()
        res_copy(zp).wait_send()
    att_copy(c).wait_send()
    for j in range(1, back + 1):

        @pl.when(h + j < nh)
        def _(j=j):
            seg_copy(j).wait_send()

        @pl.when(beside(j))
        def _(j=j):
            for g in range(heads_kv):
                kv_copy(j, g).wait_send()

    for i in range(len(relays)):

        @pl.when(relaying(i))
        def _(i=i):
            for g in range(heads_kv):
                relay_copy(i, g).wait_send()

    for half in range(3):

        @pl.when(z < nz - 1)
        def _(half=half):
            z_copy(own_piece(half), z, half, 0, 0).wait_send()

        @pl.when(z > 0)
        def _(half=half):
            z_copy(own_piece(half), z, half, 1, 0).wait_send()

    for step in range(1, nz):

        def drain(zp, way):
            for half in range(3):

                @pl.when((z < nz - 1) if way == 0 else (z > 0))
                def _(half=half):
                    z_copy(piece(zp, h, half), zp, half, way, step).wait_send()

            if nh > 1:
                sent = wbuf.at[zp, 0 : quarter * (nh - 1)]
                pltpu.make_async_copy(sent, sent, p_send.at[zp]).wait()

        both_ways(step, drain)


def on_device(ndp, nh, queries, keys_values, segment_ids, residual, out_weight):
    rows, heads, hd = queries.shape
    heads_kv = keys_values.shape[1]
    width, cols = out_weight.shape
    nz = ndp // 2
    nx = math.isqrt(nh)
    while nh % nx:
        nx -= 1
    ny = nh // nx
    back = nh // 2
    direct = 0
    for part in (width // 8, 3 * width // 16):
        if (width - part) % (16 * nh) == 0:
            direct = part
    relays = tuple(
        (j, t)
        for j in range(nx, back + 1, nx)
        for t in range(1 - nx, nx)
        if t and 1 <= j + t <= back
    )
    dims = (nz, ny, nx, back, heads, heads_kv, hd, rows, cols, width, direct, relays)
    any_spec = pl.BlockSpec(memory_space=pl.ANY)
    dma = pltpu.SemaphoreType.DMA
    bf16 = jnp.bfloat16
    return pl.pallas_call(
        functools.partial(kernel, dims),
        out_shape=jax.ShapeDtypeStruct(residual.shape, bf16),
        in_specs=[any_spec, any_spec, pl.BlockSpec(memory_space=pltpu.VMEM), any_spec, any_spec],
        out_specs=any_spec,
        scratch_shapes=[
            pltpu.VMEM((nz, width, cols), bf16),
            pltpu.VMEM((back + 1, heads_kv, rows, 2 * hd), bf16),
            pltpu.VMEM((back + 1, 8, rows), jnp.int32),
            pltpu.VMEM((rows, 128), jnp.int32),
            pltpu.VMEM((rows, heads, hd), bf16),
            pltpu.VMEM((heads, rows, hd), bf16),
            pltpu.VMEM((2 * rows, width), bf16),
            pltpu.VMEM((nz, 2 * rows, cols), bf16),
            pltpu.VMEM((nz, 2 * rows, cols), bf16),
            dma((nz, nh + 1, 2)),
            dma((2, nz, 3)),
            dma((nz,)),
            dma((back + 1, heads_kv)),
            dma((back + 1, heads_kv)),
            dma((max(1, len(relays)), heads_kv)),
            dma((back + 1,)),
            dma((back + 1,)),
            dma((nz,)),
            dma((nz,)),
            dma,
            dma,
            dma((nz,)),
            dma((nz,)),
            dma((4 + nz,)),
            dma((nz,)),
        ],
        compiler_params=pltpu.CompilerParams(
            collective_id=0, has_side_effects=True, vmem_limit_bytes=56 * 1024 * 1024
        ),
        cost_estimate=pl.CostEstimate(flops=6 * 10**9, bytes_accessed=2 * 10**7, transcendentals=3 * 10**6),
    )(
        queries,
        jnp.transpose(keys_values, (1, 0, 2)),
        segment_ids,
        residual,
        out_weight,
    )


def solution(mesh):
    return jax.shard_map(
        functools.partial(on_device, mesh.shape["dp"], mesh.shape["help"]),
        mesh=mesh,
        in_specs=(
            P(("dp", "help"), None, None),
            P(("dp", "help"), None, None),
            P("dp", "help"),
            P(("dp", "help"), None),
            P(None, "dp"),
        ),
        out_specs=P(("dp", "help"), None),
        check_vma=False,
    )
```

```python
import functools
import math

import jax
import jax.numpy as jnp
from jax import lax
from jax.experimental import pallas as pl
from jax.experimental.pallas import tpu as pltpu
from jax.sharding import PartitionSpec as P

MESH = pl.DeviceIdType.MESH
masked_score = -1e30


def kernel(
    dims,
    q_ref,
    kv_ref,
    seg_ref,
    res_ref,
    w_ref,
    out_ref,
    wbuf,
    kvbuf,
    segbuf,
    segcol,
    qraw,
    qbuf,
    att,
    resbuf,
    ost,
    w_recv,
    z_send,
    p_send,
    kv_recv,
    kv_send,
    relay_send,
    seg_recv,
    seg_send,
    res_recv,
    res_send,
    att_recv,
    att_send,
    out_recv,
    out_send,
    loc,
    loc_out,
):
    nz, ny, nx, back, heads, heads_kv, hd, rows, cols, width, direct, relays = dims
    nh = ny * nx
    quarter = (width - direct) // nh
    split = quarter // 32 * 16
    sizes = (split, quarter - split, direct)
    dp = lax.axis_index("dp")
    h = lax.axis_index("help")
    z, c = dp // 2, lax.rem(dp, 2)
    y, x = h // nx, lax.rem(h, nx)
    sib = (z * 2 + (1 - c), h)
    x_mates = [lax.rem(x + i, nx) for i in range(1, nx)]
    y_mates = [lax.rem(y + i, ny) for i in range(1, ny)]

    def column(zp, core):
        return pl.ds(pl.multiple_of((zp * 2 + core) * cols, cols), cols)

    def own_rows(core):
        return pl.ds(pl.multiple_of(core * rows, rows), rows)

    def piece(zp, hp, half):
        if half == 2:
            return wbuf.at[zp, 0:direct]
        start = pl.multiple_of(direct + hp * quarter + half * split, 16)
        return wbuf.at[zp, pl.ds(start, sizes[half])]

    def w_sem(zp, hp, half):
        return w_recv.at[zp, nh, 0] if half == 2 else w_recv.at[zp, hp, half]

    def remote(src, dst, ssem, rsem, dev):
        return pltpu.make_async_remote_copy(
            src_ref=src, dst_ref=dst, send_sem=ssem, recv_sem=rsem, device_id=dev, device_id_type=MESH
        )

    barrier = pltpu.get_barrier_semaphore()
    greet = functools.partial(pl.semaphore_signal, barrier, inc=1, device_id_type=MESH)
    greet(device_id=sib)
    for i in range(1, nh):
        greet(device_id=(dp, lax.rem(h + i, nh)))

    @pl.when(z > 0)
    def _():
        greet(device_id=(dp - 2, h))

    @pl.when(z < nz - 1)
    def _():
        greet(device_id=(dp + 2, h))

    pl.semaphore_wait(
        barrier, nh + jnp.where(z > 0, 1, 0) + jnp.where(z < nz - 1, 1, 0)
    )

    def z_copy(src, zp, half, way, step):
        dev = (dp + 2, h) if way == 0 else (dp - 2, h)
        return remote(src, piece(zp, h, half), z_send.at[way, step, half], w_sem(zp, h, half), dev)

    def own_piece(half):
        if half == 2:
            return w_ref.at[0:direct]
        start = pl.multiple_of(direct + h * quarter + half * split, 16)
        return w_ref.at[pl.ds(start, sizes[half])]

    def own_out(half):
        @pl.when(z < nz - 1)
        def _():
            z_copy(own_piece(half), z, half, 0, 0).start()

        @pl.when(z > 0)
        def _():
            z_copy(own_piece(half), z, half, 1, 0).start()

    own_out(0)
    own_out(1)

    def seg_copy(j):
        return remote(segbuf.at[0], segbuf.at[j], seg_send.at[j], seg_recv.at[j], (dp, lax.rem(h + j, nh)))

    def kv_copy(j, g):
        return remote(
            kv_ref.at[g], kvbuf.at[j, g], kv_send.at[j, g], kv_recv.at[j, g], (dp, lax.rem(h + j, nh))
        )

    def beside(j):
        if j % nx == 0:
            return h + j < nh
        return x + j < nx

    def relay_copy(i, g):
        j, t = relays[i]
        return remote(
            kvbuf.at[j, g], kvbuf.at[j + t, g], relay_send.at[i, g], kv_recv.at[j + t, g], (dp, lax.rem(h + t + nh, nh))
        )

    def relaying(i):
        j, t = relays[i]
        return (h >= j) & (x + t >= 0) & (x + t < nx)

    for g in range(heads_kv):
        for j in range(1, back + 1):

            @pl.when(beside(j))
            def _(j=j, g=g):
                kv_copy(j, g).start()

    segbuf[0] = jnp.broadcast_to(seg_ref[...], (8, rows))
    for j in range(1, back + 1):

        @pl.when(h + j < nh)
        def _(j=j):
            seg_copy(j).start()

    segcol[0] = jnp.transpose(jnp.broadcast_to(seg_ref[...], (rows, rows)))

    local = [
        pltpu.make_async_copy(q_ref, qraw, loc.at[0]),
        pltpu.make_async_copy(kv_ref, kvbuf.at[0], loc.at[1]),
        pltpu.make_async_copy(w_ref, wbuf.at[z], loc.at[3]),
    ]
    for copy in local:
        copy.start()

    def res_copy(zp):
        return remote(
            res_ref.at[:, column(zp, 1 - c)],
            resbuf.at[zp, own_rows(c)],
            res_send.at[zp],
            res_recv.at[zp],
            sib,
        )

    def res_local(zp):
        return pltpu.make_async_copy(
            res_ref.at[:, column(zp, c)], resbuf.at[zp, own_rows(c)], loc.at[4 + zp]
        )

    for zp in range(nz):
        res_copy(zp).start()
        res_local(zp).start()

    def both_ways(step, run):
        @pl.when(z >= step)
        def _():
            run(z - step, 0)

        @pl.when(z + step < nz)
        def _():
            run(z + step, 1)

    def to_x(zp, hp, half):
        for xm in x_mates:
            remote(
                piece(zp, hp, half), piece(zp, hp, half), p_send.at[zp], w_sem(zp, hp, half), (dp, y * nx + xm)
            ).start()

    def to_y(zp, hp, half):
        for ym in y_mates:
            remote(
                piece(zp, hp, half), piece(zp, hp, half), p_send.at[zp], w_sem(zp, hp, half), (dp, ym * nx + x)
            ).start()

    def arrived(zp, hp, half):
        remote(
            piece(zp, hp, half), piece(zp, hp, half), p_send.at[zp], w_sem(zp, hp, half), sib
        ).wait_recv()

    def from_z(step, half):
        def run(zp, way):
            arrived(zp, h, half)

            @pl.when((z < nz - 1) if way == 0 else (z > 0))
            def _():
                z_copy(piece(zp, h, half), zp, half, way, step).start()

            if half < 2:
                to_x(zp, h, half)
                to_y(zp, h, half)

        both_ways(step, run)

    def relay(step):
        def run(zp, way):
            for xm in x_mates:
                arrived(zp, y * nx + xm, 0)
                to_y(zp, y * nx + xm, 0)
            for ym in y_mates:
                arrived(zp, ym * nx + x, 1)
                to_x(zp, ym * nx + x, 1)

        both_ways(step, run)

    scale = math.log2(math.e) / math.sqrt(hd)
    group = heads // heads_kv
    per_chunk = 2

    def fetch(g):
        for j in range(back, 0, -1):

            @pl.when(h >= j)
            def _(j=j):
                if g == 0:
                    seg_copy(j).wait_recv()
                    segcol[j] = jnp.transpose(jnp.broadcast_to(segbuf[j, 0:1, :], (rows, rows)))
                kv_copy(j, g).wait_recv()

            for i, (held, _) in enumerate(relays):
                if held == j:

                    @pl.when(relaying(i))
                    def _(i=i):
                        relay_copy(i, g).start()

    def attend(g, first):
        if first + per_chunk >= group and g + 1 < heads_kv:
            fetch(g + 1)
        q_seg = seg_ref[...]
        here = [g * group + first + i for i in range(per_chunk)]

        def scores(head, j, allowed):
            s = lax.dot_general(
                kvbuf[j, g, :, 0:hd], qbuf[head], (((1,), (1,)), ((), ())), preferred_element_type=jnp.float32
            )
            return jnp.where(allowed, s * scale, masked_score)

        def mix(values, weights):
            return jnp.dot(values, weights.astype(jnp.bfloat16), preferred_element_type=jnp.float32)

        causal = lax.broadcasted_iota(jnp.int32, (rows, rows), 0) <= lax.broadcasted_iota(
            jnp.int32, (rows, rows), 1
        )
        own = (segcol[0] == q_seg) & causal
        values = jnp.transpose(kvbuf[0, g, :, hd:])
        states = []
        for head in here:
            s = scores(head, 0, own)
            top = jnp.max(s, axis=0, keepdims=True)
            weights = jnp.exp2(s - top)
            states.append((top, jnp.sum(weights, axis=0, keepdims=True), mix(values, weights)))

        def earlier(j, states):
            allowed = segcol[j] == q_seg
            values = jnp.transpose(kvbuf[j, g, :, hd:])
            after = []
            for head, (top, total, running) in zip(here, states):
                s = scores(head, j, allowed)
                new_top = jnp.maximum(top, jnp.max(s, axis=0, keepdims=True))
                weights = jnp.exp2(s - new_top)
                factor = jnp.exp2(top - new_top)
                total = total * factor + jnp.sum(weights, axis=0, keepdims=True)
                after.append((new_top, total, running * factor + mix(values, weights)))
            return tuple(after)

        states = lax.fori_loop(1, jnp.minimum(h, back) + 1, earlier, tuple(states))
        for head, (top, total, running) in zip(here, states):
            att[own_rows(c), head * hd : (head + 1) * hd] = jnp.transpose(running / total).astype(jnp.bfloat16)

    def att_copy(core):
        return remote(att.at[own_rows(core)], att.at[own_rows(core)], att_send, att_recv, sib)

    tile = min(256, cols)

    def out_local(zp):
        return pltpu.make_async_copy(
            ost.at[zp, own_rows(c)], out_ref.at[:, column(zp, c)], loc_out.at[zp]
        )

    def out_copy(zp, core):
        return remote(
            ost.at[zp, own_rows(1 - c)], out_ref.at[:, column(zp, core)], out_send.at[zp], out_recv.at[zp], sib
        )

    def project(zp, way):
        @pl.loop(0, cols // tile)
        def _(n):
            part = pl.ds(pl.multiple_of(n * tile, tile), tile)
            summed = jnp.dot(att[...], wbuf[zp, :, part], preferred_element_type=jnp.float32)
            ost[zp, :, part] = (resbuf[zp, :, part].astype(jnp.float32) + summed).astype(jnp.bfloat16)

        out_copy(zp, c).start()
        out_local(zp).start()

    def complete(zp):
        for xm in x_mates:
            arrived(zp, y * nx + xm, 1)
        for ym in y_mates:
            arrived(zp, ym * nx + x, 0)
        for ym in y_mates:
            for xm in x_mates:
                arrived(zp, ym * nx + xm, 0)
                arrived(zp, ym * nx + xm, 1)

    for copy in local[:2]:
        copy.wait()
    qbuf[...] = jnp.transpose(qraw[...], (1, 0, 2))
    fetch(0)
    work = [
        functools.partial(attend, g, first)
        for g in range(heads_kv)
        for first in range(0, group, per_chunk)
    ]

    def compute(count):
        for _ in range(count):
            if work:
                work.pop(0)()

    compute(1)
    for step in range(1, nz):
        from_z(step, 0)
        compute(1)
        from_z(step, 1)
        compute(1)
        if step == 2:
            own_out(2)
        if step > 1:
            relay(step - 1)
        if step > 2:
            from_z(step - 2, 2)
        compute(1)
    if nz == 2:
        own_out(2)
    compute(len(work))
    att_copy(c).start()
    for copy in local[2:]:
        copy.wait()
    for zp in range(nz):
        res_local(zp).wait()
        res_copy(zp).wait_recv()
    if nz > 2:
        from_z(nz - 2, 2)
    relay(nz - 1)
    att_copy(1 - c).wait_recv()
    project(z, 0)

    for step in range(1, nz):
        if step == nz - 1:
            from_z(step, 2)

        def run(zp, way):
            complete(zp)
            project(zp, way)

        both_ways(step, run)

    for zp in range(nz):
        out_local(zp).wait()
        out_copy(zp, c).wait_send()
        out_copy(zp, 1 - c).wait_recv()
        res_copy(zp).wait_send()
    att_copy(c).wait_send()
    for j in range(1, back + 1):

        @pl.when(h + j < nh)
        def _(j=j):
            seg_copy(j).wait_send()

        @pl.when(beside(j))
        def _(j=j):
            for g in range(heads_kv):
                kv_copy(j, g).wait_send()

    for i in range(len(relays)):

        @pl.when(relaying(i))
        def _(i=i):
            for g in range(heads_kv):
                relay_copy(i, g).wait_send()

    for half in range(3):

        @pl.when(z < nz - 1)
        def _(half=half):
            z_copy(own_piece(half), z, half, 0, 0).wait_send()

        @pl.when(z > 0)
        def _(half=half):
            z_copy(own_piece(half), z, half, 1, 0).wait_send()

    for step in range(1, nz):

        def drain(zp, way):
            for half in range(3):

                @pl.when((z < nz - 1) if way == 0 else (z > 0))
                def _(half=half):
                    z_copy(piece(zp, h, half), zp, half, way, step).wait_send()

            if nh > 1:
                sent = wbuf.at[zp, 0 : quarter * (nh - 1)]
                pltpu.make_async_copy(sent, sent, p_send.at[zp]).wait()

        both_ways(step, drain)


def on_device(ndp, nh, queries, keys_values, segment_ids, residual, out_weight):
    rows, heads, hd = queries.shape
    heads_kv = keys_values.shape[1]
    width, cols = out_weight.shape
    nz = ndp // 2
    nx = math.isqrt(nh)
    while nh % nx:
        nx -= 1
    ny = nh // nx
    back = nh // 2
    direct = 0
    for part in (width // 8, 3 * width // 16):
        if (width - part) % (16 * nh) == 0:
            direct = part
    relays = tuple(
        (j, t)
        for j in range(nx, back + 1, nx)
        for t in range(1 - nx, nx)
        if t and 1 <= j + t <= back
    )
    dims = (nz, ny, nx, back, heads, heads_kv, hd, rows, cols, width, direct, relays)
    any_spec = pl.BlockSpec(memory_space=pl.ANY)
    dma = pltpu.SemaphoreType.DMA
    bf16 = jnp.bfloat16
    return pl.pallas_call(
        functools.partial(kernel, dims),
        out_shape=jax.ShapeDtypeStruct(residual.shape, bf16),
        in_specs=[any_spec, any_spec, pl.BlockSpec(memory_space=pltpu.VMEM), any_spec, any_spec],
        out_specs=any_spec,
        scratch_shapes=[
            pltpu.VMEM((nz, width, cols), bf16),
            pltpu.VMEM((back + 1, heads_kv, rows, 2 * hd), bf16),
            pltpu.VMEM((back + 1, 8, rows), jnp.int32),
            pltpu.VMEM((back + 1, rows, rows), jnp.int32),
            pltpu.VMEM((rows, heads, hd), bf16),
            pltpu.VMEM((heads, rows, hd), bf16),
            pltpu.VMEM((2 * rows, width), bf16),
            pltpu.VMEM((nz, 2 * rows, cols), bf16),
            pltpu.VMEM((nz, 2 * rows, cols), bf16),
            dma((nz, nh + 1, 2)),
            dma((2, nz, 3)),
            dma((nz,)),
            dma((back + 1, heads_kv)),
            dma((back + 1, heads_kv)),
            dma((max(1, len(relays)), heads_kv)),
            dma((back + 1,)),
            dma((back + 1,)),
            dma((nz,)),
            dma((nz,)),
            dma,
            dma,
            dma((nz,)),
            dma((nz,)),
            dma((4 + nz,)),
            dma((nz,)),
        ],
        compiler_params=pltpu.CompilerParams(
            collective_id=0, has_side_effects=True, vmem_limit_bytes=56 * 1024 * 1024
        ),
        cost_estimate=pl.CostEstimate(flops=6 * 10**9, bytes_accessed=2 * 10**7, transcendentals=3 * 10**6),
    )(
        queries,
        jnp.transpose(keys_values, (1, 0, 2)),
        segment_ids,
        residual,
        out_weight,
    )


def solution(mesh):
    return jax.shard_map(
        functools.partial(on_device, mesh.shape["dp"], mesh.shape["help"]),
        mesh=mesh,
        in_specs=(
            P(("dp", "help"), None, None),
            P(("dp", "help"), None, None),
            P("dp", "help"),
            P(("dp", "help"), None),
            P(None, "dp"),
        ),
        out_specs=P(("dp", "help"), None),
        check_vma=False,
    )
```

```python
import functools
import math

import jax
import jax.numpy as jnp
from jax import lax
from jax.experimental import pallas as pl
from jax.experimental.pallas import tpu as pltpu
from jax.sharding import PartitionSpec as P

MESH = pl.DeviceIdType.MESH
masked_score = -1e30


def kernel(
    dims,
    q_ref,
    kv_ref,
    seg_ref,
    res_ref,
    w_ref,
    out_ref,
    wbuf,
    kvbuf,
    segbuf,
    segcol,
    qraw,
    qbuf,
    att,
    resbuf,
    ost,
    w_recv,
    z_send,
    p_send,
    kv_recv,
    kv_send,
    relay_send,
    seg_recv,
    seg_send,
    res_recv,
    res_send,
    att_recv,
    att_send,
    out_recv,
    out_send,
    loc,
    loc_out,
):
    nz, ny, nx, back, heads, heads_kv, hd, rows, cols, width, direct, relays = dims
    nh = ny * nx
    quarter = (width - direct) // nh
    split = quarter // 32 * 16
    sizes = (split, quarter - split, direct)
    dp = lax.axis_index("dp")
    h = lax.axis_index("help")
    z, c = dp // 2, lax.rem(dp, 2)
    y, x = h // nx, lax.rem(h, nx)
    sib = (z * 2 + (1 - c), h)
    x_mates = [lax.rem(x + i, nx) for i in range(1, nx)]
    y_mates = [lax.rem(y + i, ny) for i in range(1, ny)]

    def column(zp, core):
        return pl.ds(pl.multiple_of((zp * 2 + core) * cols, cols), cols)

    def own_rows(core):
        return pl.ds(pl.multiple_of(core * rows, rows), rows)

    def piece(zp, hp, half):
        if half == 2:
            return wbuf.at[zp, 0:direct]
        start = pl.multiple_of(direct + hp * quarter + half * split, 16)
        return wbuf.at[zp, pl.ds(start, sizes[half])]

    def w_sem(zp, hp, half):
        return w_recv.at[zp, nh, 0] if half == 2 else w_recv.at[zp, hp, half]

    def remote(src, dst, ssem, rsem, dev):
        return pltpu.make_async_remote_copy(
            src_ref=src, dst_ref=dst, send_sem=ssem, recv_sem=rsem, device_id=dev, device_id_type=MESH
        )

    barrier = pltpu.get_barrier_semaphore()
    greet = functools.partial(pl.semaphore_signal, barrier, inc=1, device_id_type=MESH)
    greet(device_id=sib)
    for i in range(1, nh):
        greet(device_id=(dp, lax.rem(h + i, nh)))

    @pl.when(z > 0)
    def _():
        greet(device_id=(dp - 2, h))

    @pl.when(z < nz - 1)
    def _():
        greet(device_id=(dp + 2, h))

    pl.semaphore_wait(
        barrier, nh + jnp.where(z > 0, 1, 0) + jnp.where(z < nz - 1, 1, 0)
    )

    def z_copy(src, zp, half, way, step):
        dev = (dp + 2, h) if way == 0 else (dp - 2, h)
        return remote(src, piece(zp, h, half), z_send.at[way, step, half], w_sem(zp, h, half), dev)

    def own_piece(half):
        if half == 2:
            return w_ref.at[0:direct]
        start = pl.multiple_of(direct + h * quarter + half * split, 16)
        return w_ref.at[pl.ds(start, sizes[half])]

    def own_out(half):
        @pl.when(z < nz - 1)
        def _():
            z_copy(own_piece(half), z, half, 0, 0).start()

        @pl.when(z > 0)
        def _():
            z_copy(own_piece(half), z, half, 1, 0).start()

    own_out(0)
    own_out(1)

    def seg_copy(j):
        return remote(segbuf.at[0], segbuf.at[j], seg_send.at[j], seg_recv.at[j], (dp, lax.rem(h + j, nh)))

    def kv_copy(j, g):
        return remote(
            kv_ref.at[g], kvbuf.at[j, g], kv_send.at[j, g], kv_recv.at[j, g], (dp, lax.rem(h + j, nh))
        )

    def beside(j):
        if j % nx == 0:
            return h + j < nh
        return x + j < nx

    def relay_copy(i, g):
        j, t = relays[i]
        return remote(
            kvbuf.at[j, g], kvbuf.at[j + t, g], relay_send.at[i, g], kv_recv.at[j + t, g], (dp, lax.rem(h + t + nh, nh))
        )

    def relaying(i):
        j, t = relays[i]
        return (h >= j) & (x + t >= 0) & (x + t < nx)

    for g in range(heads_kv):
        for j in range(1, back + 1):

            @pl.when(beside(j))
            def _(j=j, g=g):
                kv_copy(j, g).start()

    segbuf[0] = jnp.broadcast_to(seg_ref[...], (8, rows))
    for j in range(1, back + 1):

        @pl.when(h + j < nh)
        def _(j=j):
            seg_copy(j).start()

    segcol[0] = jnp.transpose(jnp.broadcast_to(seg_ref[...], (rows, rows)))

    local = [
        pltpu.make_async_copy(q_ref, qraw, loc.at[0]),
        pltpu.make_async_copy(kv_ref, kvbuf.at[0], loc.at[1]),
        pltpu.make_async_copy(w_ref, wbuf.at[z], loc.at[3]),
    ]
    for copy in local:
        copy.start()

    def res_copy(zp):
        return remote(
            res_ref.at[:, column(zp, 1 - c)],
            resbuf.at[zp, own_rows(c)],
            res_send.at[zp],
            res_recv.at[zp],
            sib,
        )

    def res_local(zp):
        return pltpu.make_async_copy(
            res_ref.at[:, column(zp, c)], resbuf.at[zp, own_rows(c)], loc.at[4 + zp]
        )

    for zp in range(nz):
        res_copy(zp).start()
        res_local(zp).start()

    def both_ways(step, run):
        @pl.when(z >= step)
        def _():
            run(z - step, 0)

        @pl.when(z + step < nz)
        def _():
            run(z + step, 1)

    def to_x(zp, hp, half):
        for xm in x_mates:
            remote(
                piece(zp, hp, half), piece(zp, hp, half), p_send.at[zp], w_sem(zp, hp, half), (dp, y * nx + xm)
            ).start()

    def to_y(zp, hp, half):
        for ym in y_mates:
            remote(
                piece(zp, hp, half), piece(zp, hp, half), p_send.at[zp], w_sem(zp, hp, half), (dp, ym * nx + x)
            ).start()

    def arrived(zp, hp, half):
        remote(
            piece(zp, hp, half), piece(zp, hp, half), p_send.at[zp], w_sem(zp, hp, half), sib
        ).wait_recv()

    def from_z(step, half):
        def run(zp, way):
            arrived(zp, h, half)

            @pl.when((z < nz - 1) if way == 0 else (z > 0))
            def _():
                z_copy(piece(zp, h, half), zp, half, way, step).start()

            if half < 2:
                to_x(zp, h, half)
                to_y(zp, h, half)

        both_ways(step, run)

    def relay(step):
        def run(zp, way):
            for xm in x_mates:
                arrived(zp, y * nx + xm, 0)
                to_y(zp, y * nx + xm, 0)
            for ym in y_mates:
                arrived(zp, ym * nx + x, 1)
                to_x(zp, ym * nx + x, 1)

        both_ways(step, run)

    scale = math.log2(math.e) / math.sqrt(hd)
    group = heads // heads_kv
    per_chunk = 2

    def fetch(g):
        for j in range(back, 0, -1):

            @pl.when(h >= j)
            def _(j=j):
                if g == 0:
                    seg_copy(j).wait_recv()
                    segcol[j] = jnp.transpose(jnp.broadcast_to(segbuf[j, 0:1, :], (rows, rows)))
                kv_copy(j, g).wait_recv()

            for i, (held, _) in enumerate(relays):
                if held == j:

                    @pl.when(relaying(i))
                    def _(i=i):
                        relay_copy(i, g).start()

    def attend(g, first):
        if first + per_chunk >= group and g + 1 < heads_kv:
            fetch(g + 1)
        q_seg = seg_ref[...]
        here = [g * group + first + i for i in range(per_chunk)]

        def scores(head, j, allowed):
            s = lax.dot_general(
                kvbuf[j, g, :, 0:hd], qbuf[head], (((1,), (1,)), ((), ())), preferred_element_type=jnp.float32
            )
            return jnp.where(allowed, s * scale, masked_score)

        def mix(values, weights):
            return jnp.dot(values, weights.astype(jnp.bfloat16), preferred_element_type=jnp.float32)

        causal = lax.broadcasted_iota(jnp.int32, (rows, rows), 0) <= lax.broadcasted_iota(
            jnp.int32, (rows, rows), 1
        )
        own = (segcol[0] == q_seg) & causal
        values = jnp.transpose(kvbuf[0, g, :, hd:])
        states = []
        for head in here:
            s = scores(head, 0, own)
            top = jnp.max(s, axis=0, keepdims=True)
            weights = jnp.exp2(s - top)
            states.append((top, jnp.sum(weights, axis=0, keepdims=True), mix(values, weights)))

        def earlier(j, states):
            allowed = segcol[j] == q_seg
            values = jnp.transpose(kvbuf[j, g, :, hd:])
            after = []
            for head, (top, total, running) in zip(here, states):
                s = scores(head, j, allowed)
                new_top = jnp.maximum(top, jnp.max(s, axis=0, keepdims=True))
                weights = jnp.exp2(s - new_top)
                factor = jnp.exp2(top - new_top)
                total = total * factor + jnp.sum(weights, axis=0, keepdims=True)
                after.append((new_top, total, running * factor + mix(values, weights)))
            return tuple(after)

        states = lax.fori_loop(1, jnp.minimum(h, back) + 1, earlier, tuple(states))
        for head, (top, total, running) in zip(here, states):
            att[own_rows(c), head * hd : (head + 1) * hd] = jnp.transpose(running / total).astype(jnp.bfloat16)

    def att_copy(core):
        return remote(att.at[own_rows(core)], att.at[own_rows(core)], att_send, att_recv, sib)

    tile = min(256, cols)

    def out_local(zp):
        return pltpu.make_async_copy(
            ost.at[zp, own_rows(c)], out_ref.at[:, column(zp, c)], loc_out.at[zp]
        )

    def out_copy(zp, core):
        return remote(
            ost.at[zp, own_rows(1 - c)], out_ref.at[:, column(zp, core)], out_send.at[zp], out_recv.at[zp], sib
        )

    def project(zp, way):
        @pl.loop(0, cols // tile)
        def _(n):
            part = pl.ds(pl.multiple_of(n * tile, tile), tile)
            summed = jnp.dot(att[...], wbuf[zp, :, part], preferred_element_type=jnp.float32)
            ost[zp, :, part] = (resbuf[zp, :, part].astype(jnp.float32) + summed).astype(jnp.bfloat16)

        out_copy(zp, c).start()
        out_local(zp).start()

    def complete(zp):
        for xm in x_mates:
            arrived(zp, y * nx + xm, 1)
        for ym in y_mates:
            arrived(zp, ym * nx + x, 0)
        for ym in y_mates:
            for xm in x_mates:
                arrived(zp, ym * nx + xm, 0)
                arrived(zp, ym * nx + xm, 1)

    for copy in local[:2]:
        copy.wait()
    qbuf[...] = jnp.transpose(qraw[...], (1, 0, 2))
    fetch(0)
    work = [
        functools.partial(attend, g, first)
        for g in range(heads_kv)
        for first in range(0, group, per_chunk)
    ]

    def compute(count):
        for _ in range(count):
            if work:
                work.pop(0)()

    compute(1)
    for step in range(1, nz):
        from_z(step, 0)
        compute(1)
        from_z(step, 1)
        compute(1)
        if step == 1:
            own_out(2)
        else:
            from_z(step - 1, 2)
            relay(step - 1)
        compute(1)
    compute(len(work))
    att_copy(c).start()
    for copy in local[2:]:
        copy.wait()
    for zp in range(nz):
        res_local(zp).wait()
        res_copy(zp).wait_recv()
    relay(nz - 1)
    att_copy(1 - c).wait_recv()
    project(z, 0)

    for step in range(1, nz):
        if step == nz - 1:
            from_z(step, 2)

        def run(zp, way):
            complete(zp)
            project(zp, way)

        both_ways(step, run)

    for zp in range(nz):
        out_local(zp).wait()
        out_copy(zp, c).wait_send()
        out_copy(zp, 1 - c).wait_recv()
        res_copy(zp).wait_send()
    att_copy(c).wait_send()
    for j in range(1, back + 1):

        @pl.when(h + j < nh)
        def _(j=j):
            seg_copy(j).wait_send()

        @pl.when(beside(j))
        def _(j=j):
            for g in range(heads_kv):
                kv_copy(j, g).wait_send()

    for i in range(len(relays)):

        @pl.when(relaying(i))
        def _(i=i):
            for g in range(heads_kv):
                relay_copy(i, g).wait_send()

    for half in range(3):

        @pl.when(z < nz - 1)
        def _(half=half):
            z_copy(own_piece(half), z, half, 0, 0).wait_send()

        @pl.when(z > 0)
        def _(half=half):
            z_copy(own_piece(half), z, half, 1, 0).wait_send()

    for step in range(1, nz):

        def drain(zp, way):
            for half in range(3):

                @pl.when((z < nz - 1) if way == 0 else (z > 0))
                def _(half=half):
                    z_copy(piece(zp, h, half), zp, half, way, step).wait_send()

            if nh > 1:
                sent = wbuf.at[zp, 0 : quarter * (nh - 1)]
                pltpu.make_async_copy(sent, sent, p_send.at[zp]).wait()

        both_ways(step, drain)


def on_device(ndp, nh, queries, keys_values, segment_ids, residual, out_weight):
    rows, heads, hd = queries.shape
    heads_kv = keys_values.shape[1]
    width, cols = out_weight.shape
    nz = ndp // 2
    nx = math.isqrt(nh)
    while nh % nx:
        nx -= 1
    ny = nh // nx
    back = nh // 2
    direct = width // 8
    relays = tuple(
        (j, t)
        for j in range(nx, back + 1, nx)
        for t in range(1 - nx, nx)
        if t and 1 <= j + t <= back
    )
    dims = (nz, ny, nx, back, heads, heads_kv, hd, rows, cols, width, direct, relays)
    any_spec = pl.BlockSpec(memory_space=pl.ANY)
    dma = pltpu.SemaphoreType.DMA
    bf16 = jnp.bfloat16
    return pl.pallas_call(
        functools.partial(kernel, dims),
        out_shape=jax.ShapeDtypeStruct(residual.shape, bf16),
        in_specs=[any_spec, any_spec, pl.BlockSpec(memory_space=pltpu.VMEM), any_spec, any_spec],
        out_specs=any_spec,
        scratch_shapes=[
            pltpu.VMEM((nz, width, cols), bf16),
            pltpu.VMEM((back + 1, heads_kv, rows, 2 * hd), bf16),
            pltpu.VMEM((back + 1, 8, rows), jnp.int32),
            pltpu.VMEM((back + 1, rows, rows), jnp.int32),
            pltpu.VMEM((rows, heads, hd), bf16),
            pltpu.VMEM((heads, rows, hd), bf16),
            pltpu.VMEM((2 * rows, width), bf16),
            pltpu.VMEM((nz, 2 * rows, cols), bf16),
            pltpu.VMEM((nz, 2 * rows, cols), bf16),
            dma((nz, nh + 1, 2)),
            dma((2, nz, 3)),
            dma((nz,)),
            dma((back + 1, heads_kv)),
            dma((back + 1, heads_kv)),
            dma((max(1, len(relays)), heads_kv)),
            dma((back + 1,)),
            dma((back + 1,)),
            dma((nz,)),
            dma((nz,)),
            dma,
            dma,
            dma((nz,)),
            dma((nz,)),
            dma((4 + nz,)),
            dma((nz,)),
        ],
        compiler_params=pltpu.CompilerParams(
            collective_id=0, has_side_effects=True, vmem_limit_bytes=56 * 1024 * 1024
        ),
        cost_estimate=pl.CostEstimate(flops=6 * 10**9, bytes_accessed=2 * 10**7, transcendentals=3 * 10**6),
    )(
        queries,
        jnp.transpose(keys_values, (1, 0, 2)),
        segment_ids,
        residual,
        out_weight,
    )


def solution(mesh):
    return jax.shard_map(
        functools.partial(on_device, mesh.shape["dp"], mesh.shape["help"]),
        mesh=mesh,
        in_specs=(
            P(("dp", "help"), None, None),
            P(("dp", "help"), None, None),
            P("dp", "help"),
            P(("dp", "help"), None),
            P(None, "dp"),
        ),
        out_specs=P(("dp", "help"), None),
        check_vma=False,
    )
```
